32 devices in a mesh: people: 2 (over x), tm: 8 (over z, y), type: 2 (over core).
Axes of the slice: x: 2, y: 2, z: 4, core: 2. Of those that a mesh axis runs over, the one named last changes fastest.
Arguments:
- features: bfloat16 [3, 2, 2048], P(None, 'people', 'tm'), may hold values from -6 to 6
- wear: int32 [2, 2048], P('people', 'tm'), may hold values 0 or 1
- rec_start: int32 [2], P('people'), may hold values from 0 to 255
- rec_end: int32 [2], P('people'), may hold values from 1793 to 2048
- conv_first: bfloat16 [3, 3, 128], replicated, may hold values from -2 to 2
- conv_second: bfloat16 [3, 128, 128], replicated, may hold values from -0.3125 to 0.3125
- emit_weight: bfloat16 [128, 512], P(None, 'type'), may hold values from -0.5 to 0.5
- leave: float32 [8, 64], P('type'), may hold values from 0.002 to 0.5
- jump: float32 [8, 64, 64], P('type'), may hold values from -6 to 6
- init_logits: float32 [8, 64], P('type'), may hold values from -6 to 6
- type_prior: float32 [8], replicated, may hold values from -4 to 4
Outputs:
- loglik_rate: float32 [2, 8], P('people', 'type')
- type_post: float32 [2, 8], P('people', 'type')
- occupancy: float32 [8, 64], P('type')
- filtered: float32 [2, 2048, 8, 64], P('people', 'tm', 'type')
The draws below stay inside these ranges and needn't reach their ends.
All inputs are finite; a program needn't handle non-finite values. No bound on the sum of `wear` on one device may be relied on, other than what follows from the above.
Results may differ from the reference program's by a relative error of at most 0.0085.
Values may be sent and summed in bfloat16 or wider, within the bound.
A program may use at most 64 MiB of HBM per device.

```python
import math
import jax
import jax.numpy as jnp
from jax import lax

S = 64
K = 8
C = 128
CIN = 3
EP_DEV = 256
PEOPLE = 2
NE = 2048


def touch_ends(values, stream_key, least, largest):
    shape = values.shape
    spot = [jax.random.randint(jax.random.fold_in(stream_key, axis), (), 0, shape[axis]) for axis in range(len(shape))]
    values = values.at[tuple(spot)].set(least)
    longest = shape.index(max(shape))
    spot[longest] = (spot[longest] + 1) % shape[longest]
    return values.at[tuple(spot)].set(largest)


def block_levels(stream_key, dims, split, smallest, largest):
    def one(position, shards_of):
        heights = jax.random.uniform(jax.random.fold_in(jax.random.fold_in(stream_key, 6), position), (shards_of,), jnp.float32, smallest / len(split), largest / len(split))
        return jnp.repeat(jnp.exp(heights), dims[position] // shards_of).reshape((-1,) + (1,) * (len(dims) - position - 1))

    level = one(*split[0])
    for cut in split[1:]:
        level = level * one(*cut)
    return level


def normal_values(own_key, dims, scale, limit, cuts=(), held_as=jnp.bfloat16):
    entries = scale * jax.random.normal(own_key, dims, jnp.float32)
    if cuts:
        entries = entries * block_levels(own_key, dims, cuts, -0.22, 0.18)
    return jnp.clip(entries, -limit, limit).astype(held_as)


def setup_inputs(seed: int = 0) -> dict:
    keys = jax.random.split(jax.random.key(seed), 12)
    return {
        "features": normal_values(keys[0], (CIN, PEOPLE, NE), 1.0, 6.0, ((1, 2), (2, 8))),
        "wear": touch_ends((jax.random.randint(keys[1], (PEOPLE, NE), 0, 5) < 4).astype(jnp.int32), jax.random.fold_in(keys[1], 1), 0, 1),
        "rec_start": jax.random.randint(keys[2], (PEOPLE,), 0, EP_DEV).astype(jnp.int32),
        "rec_end": jax.random.randint(keys[3], (PEOPLE,), NE - EP_DEV + 1, NE + 1).astype(jnp.int32),
        "conv_first": normal_values(keys[4], (3, CIN, C), (3 * CIN) ** -0.5, 2.0),
        "conv_second": normal_values(keys[5], (3, C, C), (3 * C) ** -0.5, 0.3125),
        "emit_weight": normal_values(keys[6], (C, K * S), C ** -0.5, 0.5, ((1, 2),)),
        "leave": jnp.clip(jnp.exp(math.log(0.5) - 5.521461 * jax.random.uniform(keys[7], (K, S), jnp.float32) ** block_levels(keys[7], (K, S), ((0, 2),), -0.2, 0.2)), 0.002, 0.5),
        "jump": normal_values(keys[8], (K, S, S), 1.0, 6.0, ((0, 2),), jnp.float32),
        "init_logits": normal_values(keys[9], (K, S), 1.0, 6.0, ((0, 2),), jnp.float32),
        "type_prior": normal_values(keys[10], (K,), 1.0, 4.0, (), jnp.float32),
    }


def conv_layer(signal, weights, dilation):
    length = signal.shape[1]
    padded = jnp.pad(signal, ((0, 0), (dilation, dilation), (0, 0)))
    total = jnp.zeros(signal.shape[:2] + (weights.shape[2],), jnp.float32)
    for tap in range(3):
        piece = padded[:, tap * dilation: tap * dilation + length, :]
        total = total + jnp.einsum('ptc,cd->ptd', piece.astype(jnp.float32), weights[tap].astype(jnp.float32))
    return total


def transitions(leave, jump):
    eye = jnp.eye(jump.shape[-1], dtype=jnp.float32)
    return (1.0 - leave)[..., None] * eye + leave[..., None] * jax.nn.softmax(jump, axis=-1)


def reference(features, wear, rec_start, rec_end, conv_first, conv_second, emit_weight, leave, jump, init_logits, type_prior):
    persons = features.shape[1]
    epochs = features.shape[2]
    kinds = jump.shape[0]
    states = jump.shape[-1]
    signal = jnp.transpose(features, (1, 2, 0))
    first = jax.nn.silu(conv_layer(signal, conv_first, 1)).astype(jnp.bfloat16)
    second = jax.nn.silu(conv_layer(first, conv_second, 4)).astype(jnp.bfloat16)
    logits = jnp.einsum('ptc,cm->ptm', second.astype(jnp.float32), emit_weight.astype(jnp.float32))
    probs = jnp.exp(jax.nn.log_softmax(logits.reshape(persons, epochs, kinds, states), axis=-1))
    steps_all = jnp.arange(epochs, dtype=jnp.int32)
    observed = (wear > 0) & (steps_all[None, :] >= rec_start[:, None]) & (steps_all[None, :] < rec_end[:, None])
    emis = jnp.where(observed[:, :, None, None], probs, jnp.float32(1.0))
    observed_f = observed.astype(jnp.float32)
    trans = transitions(leave, jump)
    start = jax.nn.softmax(init_logits, axis=-1)

    def advance(carry, inputs):
        alpha, loglik, occupied = carry
        emis_now, mask_now = inputs
        pred = jnp.einsum('pki,kij->pkj', alpha, trans, precision=lax.Precision.HIGHEST)
        unnorm = pred * emis_now
        total = jnp.sum(unnorm, axis=-1)
        alpha = unnorm / total[..., None]
        loglik = loglik + jnp.log(total)
        occupied = occupied + mask_now[:, None, None] * alpha
        return (alpha, loglik, occupied), alpha

    alpha0 = jnp.broadcast_to(start, (persons, kinds, states)).astype(jnp.float32)
    carry0 = (alpha0, jnp.zeros((persons, kinds), jnp.float32), jnp.zeros((persons, kinds, states), jnp.float32))
    (alpha, loglik, occupied), history = lax.scan(advance, carry0, (jnp.transpose(emis, (1, 0, 2, 3)), observed_f.T))
    filtered = jnp.transpose(history, (1, 0, 2, 3))
    loglik_rate = loglik / epochs
    type_post = jax.nn.softmax(type_prior[None, :] + 8.0 * loglik_rate, axis=-1)
    numer = jnp.einsum('pk,pks->ks', type_post, occupied, precision=lax.Precision.HIGHEST)
    denom = jnp.einsum('pk,p->k', type_post, jnp.sum(observed_f, axis=1), precision=lax.Precision.HIGHEST)
    occupancy = numer / denom[:, None]
    return (loglik_rate, type_post, occupancy, filtered)
```

```python
import functools

import jax
import jax.numpy as jnp
from jax import lax
from jax.experimental import pallas as pl
from jax.experimental.pallas import tpu as pltpu
from jax.sharding import PartitionSpec as P

MESH = pl.DeviceIdType.MESH
F32 = jnp.float32
BF16 = jnp.bfloat16
CHUNKS = 16


def split2(x):
    hi = x.astype(BF16)
    return hi, (x - hi.astype(F32)).astype(BF16)


def dot(a, b):
    return jnp.dot(a, b, preferred_element_type=F32)


def silu(x):
    return x / (1.0 + jnp.exp(-x))


def kernel(
    sizes,
    feat_ref,
    wear_ref,
    rs_ref,
    re_ref,
    cf_ref,
    cs_ref,
    ew_ref,
    leave_ref,
    jump_ref,
    init_ref,
    prior_ref,
    rate_ref,
    post_ref,
    occ_ref,
    filt_ref,
    fbuf,
    halo_l,
    halo_r,
    w9,
    lj,
    tcat,
    rows,
    emis,
    seen,
    x_scr,
    q_scr,
    d_own,
    d_all,
    msg,
    stats,
    halo_send,
    halo_recv,
    d_send,
    d_recv,
    s_send,
    s_recv,
):
    n_p, n_t, n_k = sizes
    span = feat_ref.shape[2]
    kinds, states = leave_ref.shape
    width = kinds * states
    halves = width // 128
    group = CHUNKS
    steps = span // group
    me_p = lax.axis_index("people")
    me_t = lax.axis_index("tm")
    me_k = lax.axis_index("type")
    others = [
        (a, b, c)
        for b in range(n_t)
        for a in range(n_p)
        for c in range(n_k)
        if (a, b, c) != (0, 0, 0)
    ]

    barrier = pltpu.get_barrier_semaphore()
    for a, b, c in others:
        pl.semaphore_signal(
            barrier,
            inc=1,
            device_id=(
                lax.rem(me_p + a, n_p),
                lax.rem(me_t + b, n_t),
                lax.rem(me_k + c, n_k),
            ),
            device_id_type=MESH,
        )

    fbuf[...] = jnp.zeros_like(fbuf)
    for i in range(feat_ref.shape[0]):
        fbuf[i : i + 1, :] = feat_ref[i].astype(F32)

    pl.semaphore_wait(barrier, len(others))
    right = lax.rem(me_t + 1, n_t)
    left = lax.rem(me_t + n_t - 1, n_t)
    to_right = pltpu.make_async_remote_copy(
        src_ref=fbuf.at[:, span - 128 : span],
        dst_ref=halo_l,
        send_sem=halo_send.at[0],
        recv_sem=halo_recv.at[0],
        device_id=(me_p, right, me_k),
        device_id_type=MESH,
    )
    to_left = pltpu.make_async_remote_copy(
        src_ref=fbuf.at[:, 0:128],
        dst_ref=halo_r,
        send_sem=halo_send.at[1],
        recv_sem=halo_recv.at[1],
        device_id=(me_p, left, me_k),
        device_id_type=MESH,
    )
    to_right.start()
    to_left.start()

    r64 = lax.broadcasted_iota(jnp.int32, (states, states), 0)
    c64 = lax.broadcasted_iota(jnp.int32, (states, states), 1)
    eye64 = r64 == c64
    rw = lax.broadcasted_iota(jnp.int32, (width, width), 0)
    cw = lax.broadcasted_iota(jnp.int32, (width, width), 1)
    ones_blk = jnp.where(rw // states == cw // states, 1.0, 0.0).astype(BF16)
    eye_cat = (
        lax.broadcasted_iota(jnp.int32, (states, width), 1) % states
        == lax.broadcasted_iota(jnp.int32, (states, width), 0)
    )

    lj[...] = jnp.zeros_like(lj)
    rows[...] = jnp.zeros_like(rows)
    for k in range(kinds):
        lanes = slice(k * states, (k + 1) * states)
        logit = jump_ref[k]
        e = jnp.exp(logit - jnp.max(logit, axis=1, keepdims=True))
        soft = e / jnp.sum(e, axis=1, keepdims=True)
        away = leave_ref[k : k + 1, :]
        away_col = jnp.sum(jnp.where(eye64, away, 0.0), axis=1, keepdims=True)
        jumped = away_col * soft
        lj[lanes, lanes] = jumped
        tcat[:, lanes] = jumped + jnp.where(eye64, 1.0 - away, 0.0)
        rows[0:1, lanes] = 1.0 - away
        first_logit = init_ref[k : k + 1, :]
        e0 = jnp.exp(first_logit - jnp.max(first_logit, axis=1, keepdims=True))
        rows[1:2, lanes] = e0 / jnp.sum(e0, axis=1, keepdims=True)
    lj_b = lj[...].astype(BF16)
    both = jnp.concatenate([lj_b, ones_blk], axis=1)
    stay = rows[0:1, :]

    def blocksum(x):
        hi, lo = split2(x)
        return dot(hi, ones_blk) + dot(lo, ones_blk)

    place = me_t * span + lax.broadcasted_iota(jnp.int32, (1, span), 1)
    seen_row = (wear_ref[...] > 0) & (place >= rs_ref[0]) & (place < re_ref[0])
    seen_row = jnp.where(seen_row, 1.0, 0.0)
    re_ = lax.broadcasted_iota(jnp.int32, (span, span), 0)
    ce_ = lax.broadcasted_iota(jnp.int32, (span, span), 1)
    seen_diag = jnp.where(re_ == ce_, seen_row, 0.0).astype(BF16)
    seen[...] = dot(seen_diag, jnp.ones((span, 128), BF16))

    w9[...] = jnp.zeros_like(w9)
    for j in range(3):
        w9[8 * j : 8 * j + cf_ref.shape[1], :] = cf_ref[j].astype(F32)

    to_right.wait()
    to_left.wait()
    before = jnp.where(me_t > 0, halo_l[...], 0.0)
    after = jnp.where(me_t < n_t - 1, halo_r[...], 0.0)
    ext = jnp.concatenate([before, fbuf[...], after], axis=1)
    wide = span + 128
    taps = jnp.concatenate([ext[:, 123 + j : 123 + j + wide] for j in range(3)], axis=0)
    first = lax.dot_general(
        taps.T.astype(BF16), w9[...].astype(BF16), (((1,), (0,)), ((), ())),
        preferred_element_type=F32,
    )
    first = silu(first[0 : span + 8])
    wpos = me_t * span - 4 + lax.broadcasted_iota(jnp.int32, first.shape, 0)
    first = jnp.where((wpos >= 0) & (wpos < span * n_t), first, 0.0)
    second = (
        dot(first[0:span].astype(BF16), cs_ref[0])
        + dot(first[4 : span + 4].astype(BF16), cs_ref[1])
        + dot(first[8 : span + 8].astype(BF16), cs_ref[2])
    )
    second = silu(second).astype(BF16)
    logits = dot(second, ew_ref[...])
    tops = [
        jnp.broadcast_to(
            jnp.max(logits[:, k * states : (k + 1) * states], axis=1, keepdims=True),
            (span, states),
        )
        for k in range(kinds)
    ]
    raw = jnp.exp(logits - jnp.concatenate(tops, axis=1))
    obs = jnp.concatenate([seen[...]] * halves, axis=1)
    log_part = -jnp.sum(obs * jnp.log(blocksum(raw)), axis=0, keepdims=True)
    raw = jnp.where(obs > 0.0, raw, 1.0)
    for h in range(halves):
        emis[h] = raw[:, h * 128 : (h + 1) * 128]

    def emission(step):
        at = pl.ds(step, group, stride=steps)
        return jnp.concatenate([emis[h, at, :] for h in range(halves)], axis=1)


    tc = tcat[...]

    def col(x):
        return jnp.sum(x.reshape(group, states, width), axis=1)

    e_first = emission(0)
    x0 = (tc[None] * e_first[:, None, :]).reshape(group * states, width)
    x_scr[...] = x0

    def grow(step, total):
        scale = 1.0 / dot(total.astype(BF16), ones_blk)
        e_now = emission(step) * scale
        x = x_scr[...]
        moved = dot(x.astype(BF16), lj_b) + x * stay
        x = (moved.reshape(group, states, width) * e_now[:, None, :]).reshape(
            group * states, width
        )
        x_scr[...] = x
        return col(x)

    total = lax.fori_loop(1, steps, grow, col(x0))

    q_scr[0] = jnp.where(eye_cat, 1.0, 0.0)
    q = x_scr[0:states, :]
    block_mask = rw // states == cw // states

    def as_block(x):
        return jnp.where(block_mask, jnp.concatenate([x] * kinds, axis=0), 0.0)

    for g in range(1, group):
        scale = 1.0 / dot(
            jnp.broadcast_to(jnp.sum(q, axis=0, keepdims=True), (8, width)).astype(BF16), ones_blk
        )
        q_scr[g] = q
        p_hi, p_lo = split2(as_block(x_scr[g * states : (g + 1) * states, :]))
        q_hi, q_lo = split2(q)
        moved = dot(jnp.concatenate([q_hi, q_lo], axis=0), p_hi)
        q = (moved[0:states] + moved[states:] + dot(q_hi, p_lo)) * scale[0:1]
    scale = 1.0 / dot(
            jnp.broadcast_to(jnp.sum(q, axis=0, keepdims=True), (8, width)).astype(BF16), ones_blk
        )
    d_own[...] = (q * scale[0:1]).astype(BF16)

    def send_operator(b):
        return pltpu.make_async_remote_copy(
            src_ref=d_own,
            dst_ref=d_all.at[me_t],
            send_sem=d_send.at[b],
            recv_sem=d_recv.at[me_t],
            device_id=(me_p, lax.rem(me_t + b, n_t), me_k),
            device_id_type=MESH,
        )

    for b in range(1, n_t):
        @pl.when(me_t + b < n_t)
        def _():
            send_operator(b).start()

    def expand(v):
        hi, lo = split2(jnp.where(eye_cat, v, 0.0))
        return dot(hi, ones_blk) + dot(lo, ones_blk)

    def apply(d, v):
        pltpu.make_async_remote_copy(
            src_ref=d_own,
            dst_ref=d_all.at[d],
            send_sem=d_send.at[0],
            recv_sem=d_recv.at[d],
            device_id=(me_p, left, me_k),
            device_id_type=MESH,
        ).wait_recv()
        spread = expand(v)
        new = jnp.sum(spread * d_all[d].astype(F32), axis=0, keepdims=True)
        return new / jnp.sum(spread, axis=0, keepdims=True)

    alpha_in = lax.fori_loop(0, me_t, apply, rows[1:2, :])

    spread = expand(alpha_in)
    alpha0 = jnp.concatenate(
        [jnp.sum(spread * q_scr[g], axis=0, keepdims=True) for g in range(group)], axis=0
    )

    def forward(u):
        hi, lo = split2(u)
        got = dot(jnp.concatenate([hi, lo], axis=0), both)
        got = got[0:group] + got[group:]
        return u * stay + got[:, :width], 1.0 / got[:, width:]

    logs = jnp.zeros((group, width), F32)
    occupied = jnp.zeros((group, width), F32)
    ahead, inv = forward(alpha0)
    for step in range(steps):
        u = ahead * inv * emission(step)
        ahead, inv = forward(u)
        alpha = u * inv
        for k in range(kinds):
            half = alpha[:, k // 2 * 128 : k // 2 * 128 + 128]
            filt_ref[pl.ds(step * kinds + k, group, stride=steps * kinds), :] = (
                half if k % 2 == 0 else pltpu.roll(half, 64, 1)
            )
        mask = seen[pl.ds(step, group, stride=steps), :]
        mask = jnp.concatenate([mask] * halves, axis=1)
        logs = logs - jnp.log(inv)
        occupied = occupied + mask * alpha

    loglik = jnp.sum(logs, axis=0, keepdims=True) + log_part
    occupied = jnp.sum(occupied, axis=0, keepdims=True)

    msg[...] = jnp.zeros_like(msg)
    for h in range(halves):
        lanes = slice(h * 128, (h + 1) * 128)
        msg[h : h + 1, :] = occupied[:, lanes]
        msg[2 + h : 3 + h, :] = loglik[:, lanes]
    count = jnp.sum(seen_row, axis=1, keepdims=True)
    msg[4:5, :] = jnp.broadcast_to(count, (1, 128))
    own = (me_p * n_k + me_k) * n_t + me_t

    def send_sums(a, b, c):
        return pltpu.make_async_remote_copy(
            src_ref=msg,
            dst_ref=stats.at[own],
            send_sem=s_send,
            recv_sem=s_recv,
            device_id=(
                lax.rem(me_p + a, n_p),
                lax.rem(me_t + b, n_t),
                lax.rem(me_k + c, n_k),
            ),
            device_id_type=MESH,
        )

    sends = [send_sums(*o) for o in others]
    for s in sends:
        s.start()
    stats[own] = msg[...]
    for b in range(1, n_t):
        @pl.when(me_t + b < n_t)
        def _():
            send_operator(b).wait_send()
    most = pl.ds(0, len(others))
    pltpu.make_async_copy(stats.at[most], stats.at[most], s_send).wait()
    pltpu.make_async_copy(stats.at[most], stats.at[most], s_recv).wait()

    sums = [
        [
            jnp.sum(stats[(p * n_k + c) * n_t : (p * n_k + c + 1) * n_t], axis=0)
            for c in range(n_k)
        ]
        for p in range(n_p)
    ]
    lane = lax.broadcasted_iota(jnp.int32, (1, 128), 1)
    epochs = float(span * n_t)

    def over_types(op, parts):
        m = functools.reduce(op, parts)
        return op(m, pltpu.roll(m, 64, 1))

    numer = [jnp.zeros((1, 128), F32) for _ in range(halves)]
    denom = [jnp.zeros((1, 128), F32) for _ in range(halves)]
    for p in range(n_p):
        rates, tempered = [], []
        for c in range(n_k):
            for h in range(halves):
                base = c * kinds + 2 * h
                rate = sums[p][c][2 + h : 3 + h, :] / epochs
                rates.append(rate)
                prior = jnp.where(lane < states, prior_ref[base], prior_ref[base + 1])
                tempered.append(prior + 8.0 * rate)
        top = over_types(jnp.maximum, tempered)
        weights = [jnp.exp(x - top) for x in tempered]
        whole = over_types(jnp.add, weights)
        for h in range(halves):
            post = functools.reduce(
                jnp.add,
                [
                    jnp.where(me_k == c, weights[c * halves + h] / whole, 0.0)
                    for c in range(n_k)
                ],
            )
            rate = functools.reduce(
                jnp.add,
                [jnp.where(me_k == c, rates[c * halves + h], 0.0) for c in range(n_k)],
            )
            occ = functools.reduce(
                jnp.add,
                [jnp.where(me_k == c, sums[p][c][h : h + 1, :], 0.0) for c in range(n_k)],
            )
            numer[h] = numer[h] + post * occ
            denom[h] = denom[h] + post * sums[p][0][4:5, :]
            rows[2 + h : 3 + h, 0:128] = jnp.where(me_p == p, rate, rows[2 + h : 3 + h, 0:128])
            rows[4 + h : 5 + h, 0:128] = jnp.where(me_p == p, post, rows[4 + h : 5 + h, 0:128])
    for k in range(kinds):
        h, at = k // 2, (k % 2) * states
        rate_ref[0:1, k : k + 1] = rows[2 + h : 3 + h, at : at + 1]
        post_ref[0:1, k : k + 1] = rows[4 + h : 5 + h, at : at + 1]
        occ_ref[k : k + 1, :] = (numer[h] / denom[h])[:, at : at + states]


def on_device(sizes, features, *rest):
    jump = rest[7]
    kinds, states = jump.shape[0], jump.shape[2]
    span = features.shape[2]
    width = kinds * states
    n_p, n_t, n_k = sizes
    vmem = pl.BlockSpec(memory_space=pltpu.VMEM)
    smem = pl.BlockSpec(memory_space=pltpu.SMEM)
    rate, post, occ, filt = pl.pallas_call(
        functools.partial(kernel, sizes),
        out_shape=(
            jax.ShapeDtypeStruct((1, kinds), F32),
            jax.ShapeDtypeStruct((1, kinds), F32),
            jax.ShapeDtypeStruct((kinds, states), F32),
            jax.ShapeDtypeStruct((span * kinds, 128), F32),
        ),
        in_specs=[vmem, vmem, smem, smem, vmem, vmem, vmem, vmem, vmem, vmem, smem],
        out_specs=(vmem, vmem, vmem, vmem),
        scratch_shapes=[
            pltpu.VMEM((8, span), F32),
            pltpu.VMEM((8, 128), F32),
            pltpu.VMEM((8, 128), F32),
            pltpu.VMEM((24, 128), F32),
            pltpu.VMEM((width, width), F32),
            pltpu.VMEM((states, width), F32),
            pltpu.VMEM((8, width), F32),
            pltpu.VMEM((width // 128, span, 128), F32),
            pltpu.VMEM((span, 128), F32),
            pltpu.VMEM((CHUNKS * states, width), F32),
            pltpu.VMEM((CHUNKS, states, width), F32),
            pltpu.VMEM((states, width), BF16),
            pltpu.VMEM((n_t, states, width), BF16),
            pltpu.VMEM((8, 128), F32),
            pltpu.VMEM((n_p * n_t * n_k, 8, 128), F32),
            pltpu.SemaphoreType.DMA((2,)),
            pltpu.SemaphoreType.DMA((2,)),
            pltpu.SemaphoreType.DMA((n_t,)),
            pltpu.SemaphoreType.DMA((n_t,)),
            pltpu.SemaphoreType.DMA,
            pltpu.SemaphoreType.DMA,
        ],
        compiler_params=pltpu.CompilerParams(
            collective_id=0, has_side_effects=True, vmem_limit_bytes=40 * 1024 * 1024
        ),
    )(features, *rest)
    return rate, post, occ, filt[:, :states].reshape(1, span, kinds, states)


def solution(mesh):
    sizes = (mesh.shape["people"], mesh.shape["tm"], mesh.shape["type"])
    return jax.shard_map(
        functools.partial(on_device, sizes),
        mesh=mesh,
        in_specs=(
            P(None, "people", "tm"),
            P("people", "tm"),
            P("people"),
            P("people"),
            P(),
            P(),
            P(None, "type"),
            P("type", None),
            P("type", None, None),
            P("type", None),
            P(),
        ),
        out_specs=(
            P("people", "type"),
            P("people", "type"),
            P("type", None),
            P("people", "tm", "type", None),
        ),
        check_vma=False,
    )
```

```python
import functools

import jax
import jax.numpy as jnp
from jax import lax
from jax.experimental import pallas as pl
from jax.experimental.pallas import tpu as pltpu
from jax.sharding import PartitionSpec as P

MESH = pl.DeviceIdType.MESH
F32 = jnp.float32
BF16 = jnp.bfloat16
CHUNKS = 16


def split2(x):
    hi = x.astype(BF16)
    return hi, (x - hi.astype(F32)).astype(BF16)


def dot(a, b):
    return jnp.dot(a, b, preferred_element_type=F32)


def silu(x):
    return x / (1.0 + jnp.exp(-x))


def kernel(
    sizes,
    feat_ref,
    wear_ref,
    rs_ref,
    re_ref,
    cf_ref,
    cs_any,
    ew_any,
    leave_ref,
    jump_any,
    init_ref,
    prior_ref,
    rate_ref,
    post_ref,
    occ_ref,
    filt_ref,
    fbuf,
    halo_l,
    halo_r,
    w9,
    lj,
    tcat,
    rows,
    emis,
    seen,
    x_scr,
    q_scr,
    d_own,
    d_all,
    msg,
    stats,
    halo_send,
    halo_recv,
    d_send,
    d_recv,
    s_send,
    s_recv,
    cs_ref,
    ew_ref,
    jump_ref,
    loads,
):
    n_p, n_t, n_k = sizes
    span = feat_ref.shape[2]
    kinds, states = leave_ref.shape
    width = kinds * states
    halves = width // 128
    group = CHUNKS
    steps = span // group
    me_p = lax.axis_index("people")
    me_t = lax.axis_index("tm")
    me_k = lax.axis_index("type")
    others = [
        (a, b, c)
        for b in range(n_t)
        for a in range(n_p)
        for c in range(n_k)
        if (a, b, c) != (0, 0, 0)
    ]

    fetch_jump = pltpu.make_async_copy(jump_any, jump_ref, loads.at[0])
    fetch_cs = pltpu.make_async_copy(cs_any, cs_ref, loads.at[1])
    fetch_ew = pltpu.make_async_copy(ew_any, ew_ref, loads.at[2])
    fetch_jump.start()
    fetch_cs.start()
    fetch_ew.start()

    barrier = pltpu.get_barrier_semaphore()
    for a, b, c in others:
        pl.semaphore_signal(
            barrier,
            inc=1,
            device_id=(
                lax.rem(me_p + a, n_p),
                lax.rem(me_t + b, n_t),
                lax.rem(me_k + c, n_k),
            ),
            device_id_type=MESH,
        )

    fbuf[...] = jnp.zeros_like(fbuf)
    for i in range(feat_ref.shape[0]):
        fbuf[i : i + 1, :] = feat_ref[i].astype(F32)

    pl.semaphore_wait(barrier, len(others))
    right = lax.rem(me_t + 1, n_t)
    left = lax.rem(me_t + n_t - 1, n_t)
    to_right = pltpu.make_async_remote_copy(
        src_ref=fbuf.at[:, span - 128 : span],
        dst_ref=halo_l,
        send_sem=halo_send.at[0],
        recv_sem=halo_recv.at[0],
        device_id=(me_p, right, me_k),
        device_id_type=MESH,
    )
    to_left = pltpu.make_async_remote_copy(
        src_ref=fbuf.at[:, 0:128],
        dst_ref=halo_r,
        send_sem=halo_send.at[1],
        recv_sem=halo_recv.at[1],
        device_id=(me_p, left, me_k),
        device_id_type=MESH,
    )
    to_right.start()
    to_left.start()

    r64 = lax.broadcasted_iota(jnp.int32, (states, states), 0)
    c64 = lax.broadcasted_iota(jnp.int32, (states, states), 1)
    eye64 = r64 == c64
    rw = lax.broadcasted_iota(jnp.int32, (width, width), 0)
    cw = lax.broadcasted_iota(jnp.int32, (width, width), 1)
    ones_blk = jnp.where(rw // states == cw // states, 1.0, 0.0).astype(BF16)
    eye_cat = (
        lax.broadcasted_iota(jnp.int32, (states, width), 1) % states
        == lax.broadcasted_iota(jnp.int32, (states, width), 0)
    )

    lj[...] = jnp.zeros_like(lj)
    rows[...] = jnp.zeros_like(rows)
    fetch_jump.wait()
    for k in range(kinds):
        lanes = slice(k * states, (k + 1) * states)
        logit = jump_ref[k]
        e = jnp.exp(logit - jnp.max(logit, axis=1, keepdims=True))
        soft = e / jnp.sum(e, axis=1, keepdims=True)
        away = leave_ref[k : k + 1, :]
        away_col = jnp.sum(jnp.where(eye64, away, 0.0), axis=1, keepdims=True)
        jumped = away_col * soft
        lj[lanes, lanes] = jumped
        tcat[:, lanes] = jumped + jnp.where(eye64, 1.0 - away, 0.0)
        rows[0:1, lanes] = 1.0 - away
        first_logit = init_ref[k : k + 1, :]
        e0 = jnp.exp(first_logit - jnp.max(first_logit, axis=1, keepdims=True))
        rows[1:2, lanes] = e0 / jnp.sum(e0, axis=1, keepdims=True)
    lj_b = lj[...].astype(BF16)
    both = jnp.concatenate([lj_b, ones_blk], axis=1)
    stay = rows[0:1, :]

    def blocksum(x):
        hi, lo = split2(x)
        return dot(hi, ones_blk) + dot(lo, ones_blk)

    place = me_t * span + lax.broadcasted_iota(jnp.int32, (1, span), 1)
    seen_row = (wear_ref[...] > 0) & (place >= rs_ref[0]) & (place < re_ref[0])
    seen_row = jnp.where(seen_row, 1.0, 0.0)
    re_ = lax.broadcasted_iota(jnp.int32, (span, span), 0)
    ce_ = lax.broadcasted_iota(jnp.int32, (span, span), 1)
    seen_diag = jnp.where(re_ == ce_, seen_row, 0.0).astype(BF16)
    seen[...] = dot(seen_diag, jnp.ones((span, 128), BF16))

    w9[...] = jnp.zeros_like(w9)
    for j in range(3):
        w9[8 * j : 8 * j + cf_ref.shape[1], :] = cf_ref[j].astype(F32)

    fetch_cs.wait()
    fetch_ew.wait()
    to_right.wait()
    to_left.wait()
    before = jnp.where(me_t > 0, halo_l[...], 0.0)
    after = jnp.where(me_t < n_t - 1, halo_r[...], 0.0)
    ext = jnp.concatenate([before, fbuf[...], after], axis=1)
    wide = span + 128
    taps = jnp.concatenate([ext[:, 123 + j : 123 + j + wide] for j in range(3)], axis=0)
    first = lax.dot_general(
        taps.T.astype(BF16), w9[...].astype(BF16), (((1,), (0,)), ((), ())),
        preferred_element_type=F32,
    )
    first = silu(first[0 : span + 8])
    wpos = me_t * span - 4 + lax.broadcasted_iota(jnp.int32, first.shape, 0)
    first = jnp.where((wpos >= 0) & (wpos < span * n_t), first, 0.0)
    second = (
        dot(first[0:span].astype(BF16), cs_ref[0])
        + dot(first[4 : span + 4].astype(BF16), cs_ref[1])
        + dot(first[8 : span + 8].astype(BF16), cs_ref[2])
    )
    second = silu(second).astype(BF16)
    logits = dot(second, ew_ref[...])
    tops = [
        jnp.broadcast_to(
            jnp.max(logits[:, k * states : (k + 1) * states], axis=1, keepdims=True),
            (span, states),
        )
        for k in range(kinds)
    ]
    raw = jnp.exp(logits - jnp.concatenate(tops, axis=1))
    obs = jnp.concatenate([seen[...]] * halves, axis=1)
    log_part = -jnp.sum(obs * jnp.log(blocksum(raw)), axis=0, keepdims=True)
    raw = jnp.where(obs > 0.0, raw, 1.0)
    for h in range(halves):
        emis[h] = raw[:, h * 128 : (h + 1) * 128]

    def emission(step):
        at = pl.ds(step, group, stride=steps)
        return jnp.concatenate([emis[h, at, :] for h in range(halves)], axis=1)


    tc = tcat[...]

    def col(x):
        return jnp.sum(x.reshape(group, states, width), axis=1)

    e_first = emission(0)
    x0 = (tc[None] * e_first[:, None, :]).reshape(group * states, width)
    x_scr[...] = x0

    def grow(step, total):
        scale = 1.0 / dot(total.astype(BF16), ones_blk)
        e_now = emission(step) * scale
        x = x_scr[...]
        moved = dot(x.astype(BF16), lj_b) + x * stay
        x = (moved.reshape(group, states, width) * e_now[:, None, :]).reshape(
            group * states, width
        )
        x_scr[...] = x
        return col(x)

    total = lax.fori_loop(1, steps, grow, col(x0))

    q_scr[0] = jnp.where(eye_cat, 1.0, 0.0)
    q = x_scr[0:states, :]
    block_mask = rw // states == cw // states

    def as_block(x):
        return jnp.where(block_mask, jnp.concatenate([x] * kinds, axis=0), 0.0)

    for g in range(1, group):
        scale = 1.0 / dot(
            jnp.broadcast_to(jnp.sum(q, axis=0, keepdims=True), (8, width)).astype(BF16), ones_blk
        )
        q_scr[g] = q
        p_hi, p_lo = split2(as_block(x_scr[g * states : (g + 1) * states, :]))
        q_hi, q_lo = split2(q)
        moved = dot(jnp.concatenate([q_hi, q_lo], axis=0), p_hi)
        q = (moved[0:states] + moved[states:] + dot(q_hi, p_lo)) * scale[0:1]
    scale = 1.0 / dot(
            jnp.broadcast_to(jnp.sum(q, axis=0, keepdims=True), (8, width)).astype(BF16), ones_blk
        )
    d_own[...] = (q * scale[0:1]).astype(BF16)

    def send_operator(b):
        return pltpu.make_async_remote_copy(
            src_ref=d_own,
            dst_ref=d_all.at[me_t],
            send_sem=d_send.at[b],
            recv_sem=d_recv.at[me_t],
            device_id=(me_p, lax.rem(me_t + b, n_t), me_k),
            device_id_type=MESH,
        )

    for b in range(1, n_t):
        @pl.when(me_t + b < n_t)
        def _():
            send_operator(b).start()

    def expand(v):
        hi, lo = split2(jnp.where(eye_cat, v, 0.0))
        return dot(hi, ones_blk) + dot(lo, ones_blk)

    def apply(d, v):
        pltpu.make_async_remote_copy(
            src_ref=d_own,
            dst_ref=d_all.at[d],
            send_sem=d_send.at[0],
            recv_sem=d_recv.at[d],
            device_id=(me_p, left, me_k),
            device_id_type=MESH,
        ).wait_recv()
        spread = expand(v)
        new = jnp.sum(spread * d_all[d].astype(F32), axis=0, keepdims=True)
        return new / jnp.sum(spread, axis=0, keepdims=True)

    alpha_in = lax.fori_loop(0, me_t, apply, rows[1:2, :])

    spread = expand(alpha_in)
    alpha0 = jnp.concatenate(
        [jnp.sum(spread * q_scr[g], axis=0, keepdims=True) for g in range(group)], axis=0
    )

    def forward(u):
        hi, lo = split2(u)
        got = dot(jnp.concatenate([hi, lo], axis=0), both)
        got = got[0:group] + got[group:]
        return u * stay + got[:, :width], 1.0 / got[:, width:]

    logs = jnp.zeros((group, width), F32)
    occupied = jnp.zeros((group, width), F32)
    ahead, inv = forward(alpha0)
    for step in range(steps):
        u = ahead * inv * emission(step)
        ahead, inv = forward(u)
        alpha = u * inv
        for k in range(kinds):
            half = alpha[:, k // 2 * 128 : k // 2 * 128 + 128]
            filt_ref[pl.ds(step * kinds + k, group, stride=steps * kinds), :] = (
                half if k % 2 == 0 else pltpu.roll(half, 64, 1)
            )
        mask = seen[pl.ds(step, group, stride=steps), :]
        mask = jnp.concatenate([mask] * halves, axis=1)
        logs = logs - jnp.log(inv)
        occupied = occupied + mask * alpha

    loglik = jnp.sum(logs, axis=0, keepdims=True) + log_part
    occupied = jnp.sum(occupied, axis=0, keepdims=True)

    msg[...] = jnp.zeros_like(msg)
    for h in range(halves):
        lanes = slice(h * 128, (h + 1) * 128)
        msg[h : h + 1, :] = occupied[:, lanes]
        msg[2 + h : 3 + h, :] = loglik[:, lanes]
    count = jnp.sum(seen_row, axis=1, keepdims=True)
    msg[4:5, :] = jnp.broadcast_to(count, (1, 128))
    own = (me_p * n_k + me_k) * n_t + me_t

    def send_sums(a, b, c):
        return pltpu.make_async_remote_copy(
            src_ref=msg,
            dst_ref=stats.at[own],
            send_sem=s_send,
            recv_sem=s_recv,
            device_id=(
                lax.rem(me_p + a, n_p),
                lax.rem(me_t + b, n_t),
                lax.rem(me_k + c, n_k),
            ),
            device_id_type=MESH,
        )

    sends = [send_sums(*o) for o in others]
    for s in sends:
        s.start()
    stats[own] = msg[...]
    for b in range(1, n_t):
        @pl.when(me_t + b < n_t)
        def _():
            send_operator(b).wait_send()
    most = pl.ds(0, len(others))
    pltpu.make_async_copy(stats.at[most], stats.at[most], s_send).wait()
    pltpu.make_async_copy(stats.at[most], stats.at[most], s_recv).wait()

    sums = [
        [
            jnp.sum(stats[(p * n_k + c) * n_t : (p * n_k + c + 1) * n_t], axis=0)
            for c in range(n_k)
        ]
        for p in range(n_p)
    ]
    lane = lax.broadcasted_iota(jnp.int32, (1, 128), 1)
    epochs = float(span * n_t)

    def over_types(op, parts):
        m = functools.reduce(op, parts)
        return op(m, pltpu.roll(m, 64, 1))

    numer = [jnp.zeros((1, 128), F32) for _ in range(halves)]
    denom = [jnp.zeros((1, 128), F32) for _ in range(halves)]
    for p in range(n_p):
        rates, tempered = [], []
        for c in range(n_k):
            for h in range(halves):
                base = c * kinds + 2 * h
                rate = sums[p][c][2 + h : 3 + h, :] / epochs
                rates.append(rate)
                prior = jnp.where(lane < states, prior_ref[base], prior_ref[base + 1])
                tempered.append(prior + 8.0 * rate)
        top = over_types(jnp.maximum, tempered)
        weights = [jnp.exp(x - top) for x in tempered]
        whole = over_types(jnp.add, weights)
        for h in range(halves):
            post = functools.reduce(
                jnp.add,
                [
                    jnp.where(me_k == c, weights[c * halves + h] / whole, 0.0)
                    for c in range(n_k)
                ],
            )
            rate = functools.reduce(
                jnp.add,
                [jnp.where(me_k == c, rates[c * halves + h], 0.0) for c in range(n_k)],
            )
            occ = functools.reduce(
                jnp.add,
                [jnp.where(me_k == c, sums[p][c][h : h + 1, :], 0.0) for c in range(n_k)],
            )
            numer[h] = numer[h] + post * occ
            denom[h] = denom[h] + post * sums[p][0][4:5, :]
            rows[2 + h : 3 + h, 0:128] = jnp.where(me_p == p, rate, rows[2 + h : 3 + h, 0:128])
            rows[4 + h : 5 + h, 0:128] = jnp.where(me_p == p, post, rows[4 + h : 5 + h, 0:128])
    for k in range(kinds):
        h, at = k // 2, (k % 2) * states
        rate_ref[0:1, k : k + 1] = rows[2 + h : 3 + h, at : at + 1]
        post_ref[0:1, k : k + 1] = rows[4 + h : 5 + h, at : at + 1]
        occ_ref[k : k + 1, :] = (numer[h] / denom[h])[:, at : at + states]


def on_device(sizes, features, *rest):
    jump = rest[7]
    kinds, states = jump.shape[0], jump.shape[2]
    span = features.shape[2]
    width = kinds * states
    n_p, n_t, n_k = sizes
    vmem = pl.BlockSpec(memory_space=pltpu.VMEM)
    hbm = pl.BlockSpec(memory_space=pl.ANY)
    smem = pl.BlockSpec(memory_space=pltpu.SMEM)
    rate, post, occ, filt = pl.pallas_call(
        functools.partial(kernel, sizes),
        out_shape=(
            jax.ShapeDtypeStruct((1, kinds), F32),
            jax.ShapeDtypeStruct((1, kinds), F32),
            jax.ShapeDtypeStruct((kinds, states), F32),
            jax.ShapeDtypeStruct((span * kinds, 128), F32),
        ),
        in_specs=[vmem, vmem, smem, smem, vmem, hbm, hbm, vmem, hbm, vmem, smem],
        out_specs=(vmem, vmem, vmem, vmem),
        scratch_shapes=[
            pltpu.VMEM((8, span), F32),
            pltpu.VMEM((8, 128), F32),
            pltpu.VMEM((8, 128), F32),
            pltpu.VMEM((24, 128), F32),
            pltpu.VMEM((width, width), F32),
            pltpu.VMEM((states, width), F32),
            pltpu.VMEM((8, width), F32),
            pltpu.VMEM((width // 128, span, 128), F32),
            pltpu.VMEM((span, 128), F32),
            pltpu.VMEM((CHUNKS * states, width), F32),
            pltpu.VMEM((CHUNKS, states, width), F32),
            pltpu.VMEM((states, width), BF16),
            pltpu.VMEM((n_t, states, width), BF16),
            pltpu.VMEM((8, 128), F32),
            pltpu.VMEM((n_p * n_t * n_k, 8, 128), F32),
            pltpu.SemaphoreType.DMA((2,)),
            pltpu.SemaphoreType.DMA((2,)),
            pltpu.SemaphoreType.DMA((n_t,)),
            pltpu.SemaphoreType.DMA((n_t,)),
            pltpu.SemaphoreType.DMA,
            pltpu.SemaphoreType.DMA,
            pltpu.VMEM(rest[4].shape, BF16),
            pltpu.VMEM(rest[5].shape, BF16),
            pltpu.VMEM(jump.shape, F32),
            pltpu.SemaphoreType.DMA((3,)),
        ],
        compiler_params=pltpu.CompilerParams(
            collective_id=0, has_side_effects=True, vmem_limit_bytes=40 * 1024 * 1024
        ),
    )(features, *rest)
    return rate, post, occ, filt[:, :states].reshape(1, span, kinds, states)


def solution(mesh):
    sizes = (mesh.shape["people"], mesh.shape["tm"], mesh.shape["type"])
    return jax.shard_map(
        functools.partial(on_device, sizes),
        mesh=mesh,
        in_specs=(
            P(None, "people", "tm"),
            P("people", "tm"),
            P("people"),
            P("people"),
            P(),
            P(),
            P(None, "type"),
            P("type", None),
            P("type", None, None),
            P("type", None),
            P(),
        ),
        out_specs=(
            P("people", "type"),
            P("people", "type"),
            P("type", None),
            P("people", "tm", "type", None),
        ),
        check_vma=False,
    )
```
